32 devices in a mesh: gx: 16 (over z, y, core), gy: 2 (over x).
Axes of the slice: x: 2, y: 2, z: 4, core: 2. Of those that a mesh axis runs over, the one named last changes fastest.
Arguments:
- velocity_x: bfloat16 [256, 128, 128], P('gx', 'gy'), may hold values from -6 to 6
- velocity_y: bfloat16 [256, 128, 128], P('gx', 'gy'), may hold values from -6 to 6
- velocity_z: bfloat16 [256, 128, 128], P('gx', 'gy'), may hold values from -6 to 6
- potential_temp: bfloat16 [256, 128, 128], P('gx', 'gy'), may hold values from -6 to 6
- total_water: bfloat16 [256, 128, 128], P('gx', 'gy'), may hold values from -6 to 6
Outputs:
- wind_x_next: bfloat16 [256, 128, 128], P('gx', 'gy')
- wind_y_next: bfloat16 [256, 128, 128], P('gx', 'gy')
- wind_z_next: bfloat16 [256, 128, 128], P('gx', 'gy')
- temp_next: bfloat16 [256, 128, 128], P('gx', 'gy')
- water_next: bfloat16 [256, 128, 128], P('gx', 'gy')
- pressure: float32 [256, 128, 128], P('gx', 'gy')
The draws below stay inside these ranges and needn't reach their ends.
All inputs are finite; a program needn't handle non-finite values.
Results may differ from the reference program's by a relative error of at most 0.001.
Values may be sent and summed in bfloat16 or wider, within the bound.
A program may use at most 64 MiB of HBM per device.

```python
import math
import jax
import jax.numpy as jnp
from jax import lax

NZ = 128
NX = 256
NY = 128


def level_of(rng, shape, cuts, smallest, largest):
    factor_of = 1.0
    for dim, parts in cuts:
        steps = jax.random.uniform(jax.random.fold_in(jax.random.fold_in(rng, 6), dim), (parts,), jnp.float32, smallest / len(cuts), largest / len(cuts))
        factor_of = factor_of * jnp.repeat(jnp.exp(steps), shape[dim] // parts).reshape((-1,) + (1,) * (len(shape) - 1 - dim))
    return factor_of


def scatter_about(rng, extent, scale, most, pieces=(), kind=jnp.bfloat16):
    values = scale * jax.random.normal(rng, extent, jnp.float32)
    if pieces:
        values = values * level_of(rng, extent, pieces, -0.22, 0.18)
    return jnp.clip(values, -most, most).astype(kind)


def setup_inputs(seed: int = 0) -> dict:
    streams_of = jax.random.split(jax.random.key(seed), 6)
    return {
        "velocity_x": scatter_about(streams_of[0], (NX, NY, NZ), 1.0, 6.0, ((0, 16), (1, 2))),
        "velocity_y": scatter_about(streams_of[1], (NX, NY, NZ), 1.0, 6.0, ((0, 16), (1, 2))),
        "velocity_z": scatter_about(streams_of[2], (NX, NY, NZ), 1.0, 6.0, ((0, 16), (1, 2))),
        "potential_temp": scatter_about(streams_of[3], (NX, NY, NZ), 1.0, 6.0, ((0, 16), (1, 2))),
        "total_water": scatter_about(streams_of[4], (NX, NY, NZ), 1.0, 6.0, ((0, 16), (1, 2))),
    }


time_step = 0.25
diffusion = 0.1
central_coef = (-1.0, 9.0, -45.0, 0.0, 45.0, -9.0, 1.0)
damping_coef = (1.0, -6.0, 15.0, -20.0, 15.0, -6.0, 1.0)

def tendency(padded_field, speed_x, speed_y, speed_z):
    extent_x, extent_y, levels = speed_x.shape
    extended = jnp.pad(padded_field, ((0, 0), (0, 0), (3, 3)))

    def neighbour(shift_x, shift_y, shift_z):
        return extended[3 + shift_x:3 + shift_x + extent_x, 3 + shift_y:3 + shift_y + extent_y, 3 + shift_z:3 + shift_z + levels]
    centre = neighbour(0, 0, 0)
    laplace = -6.0 * centre
    advect = jnp.zeros_like(centre)
    for direction, speed in enumerate((speed_x, speed_y, speed_z)):
        central = jnp.zeros_like(centre)
        damped = jnp.zeros_like(centre)
        for offset in range(-3, 4):
            shifts = [0, 0, 0]
            shifts[direction] = offset
            sample = neighbour(shifts[0], shifts[1], shifts[2])
            central = central + central_coef[offset + 3] * sample
            damped = damped + damping_coef[offset + 3] * sample
            if offset == -1 or offset == 1:
                laplace = laplace + sample
        advect = advect + speed * central / 60.0 - jnp.abs(speed) * damped / 60.0
    return diffusion * laplace - advect

def divergence(extended_x, extended_y, vertical):
    grad_x = (extended_x[2:, 1:-1] - extended_x[:-2, 1:-1]) * 0.5
    grad_y = (extended_y[1:-1, 2:] - extended_y[1:-1, :-2]) * 0.5
    padded_z = jnp.pad(vertical, ((0, 0), (0, 0), (1, 1)))
    grad_z = (padded_z[:, :, 2:] - padded_z[:, :, :-2]) * 0.5
    return (grad_x + grad_y + grad_z) / time_step

def cosine_table(length):
    grid_index = jnp.arange(length, dtype=jnp.int32)[:, None]
    mode_index = jnp.arange(length, dtype=jnp.int32)[None, :]
    angle = math.pi / (2.0 * length) * (mode_index * (2 * grid_index + 1) % (4 * length)).astype(jnp.float32)
    scaling = jnp.where(mode_index == 0, math.sqrt(1.0 / length), math.sqrt(2.0 / length))
    return jnp.cos(angle) * scaling

def cosine_eigen(mode_index, length):
    return 2.0 * jnp.cos(math.pi / length * mode_index.astype(jnp.float32)) - 2.0

def periodic_eigen(mode_index, length):
    return 2.0 * jnp.cos(2.0 * math.pi / length * mode_index.astype(jnp.float32)) - 2.0

def pad_wrap(field, width):
    return jnp.pad(field, ((width, width), (width, width), (0, 0)), mode='wrap')

def reference(velocity_x, velocity_y, velocity_z, potential_temp, total_water):
    fields = [item.astype(jnp.float32) for item in (velocity_x, velocity_y, velocity_z, potential_temp, total_water)]
    starred = []
    for position in range(5):
        change = tendency(pad_wrap(fields[position], 3), fields[0], fields[1], fields[2])
        if position == 2:
            change = change + fields[3]
        starred.append(fields[position] + time_step * change)
    source = divergence(pad_wrap(starred[0], 1), pad_wrap(starred[1], 1), starred[2])
    table_z = cosine_table(NZ)
    coeff = jnp.dot(source.reshape(-1, NZ), table_z, precision=lax.Precision.HIGHEST).reshape(NX, NY, NZ)
    spectrum = jnp.fft.rfft2(coeff, axes=(0, 1))
    mode_x = jnp.arange(NX, dtype=jnp.int32)
    mode_y = jnp.arange(NY // 2 + 1, dtype=jnp.int32)
    mode_z = jnp.arange(NZ, dtype=jnp.int32)
    eigen = periodic_eigen(mode_x, NX)[:, None, None] + periodic_eigen(mode_y, NY)[None, :, None] + cosine_eigen(mode_z, NZ)[None, None, :]
    constant = (mode_x == 0)[:, None, None] & (mode_y == 0)[None, :, None] & (mode_z == 0)[None, None, :]
    factor = jnp.where(constant, 0.0, 1.0 / jnp.where(constant, 1.0, eigen))
    solved = jnp.fft.irfft2(spectrum * factor, s=(NX, NY), axes=(0, 1)).astype(jnp.float32)
    pressure = jnp.dot(solved.reshape(-1, NZ), table_z.T, precision=lax.Precision.HIGHEST).reshape(NX, NY, NZ)
    return (starred[0].astype(jnp.bfloat16), starred[1].astype(jnp.bfloat16), starred[2].astype(jnp.bfloat16), starred[3].astype(jnp.bfloat16), starred[4].astype(jnp.bfloat16), pressure)
```

```python
import functools
import math

import jax
import jax.numpy as jnp
import ml_dtypes
import numpy as np
from jax import lax
from jax.experimental import pallas as pl
from jax.experimental.pallas import tpu as pltpu
from jax.sharding import PartitionSpec as P

time_step = 0.25
diffusion = 0.1
f32 = jnp.float32
bf16 = jnp.bfloat16
MESH = pl.DeviceIdType.MESH


def split_table(table):
    high = table.astype(ml_dtypes.bfloat16)
    low = (table - high.astype(np.float64)).astype(ml_dtypes.bfloat16)
    return high, low


def cosine_table(length):
    grid = np.arange(length)[:, None]
    mode = np.arange(length)[None, :]
    scaling = np.where(mode == 0, math.sqrt(1.0 / length), math.sqrt(2.0 / length))
    return np.cos(math.pi / (2.0 * length) * (mode * (2 * grid + 1) % (4 * length))) * scaling


def fourier_table(length):
    grid = np.arange(length)[:, None]
    mode = np.arange(length)[None, :]
    half = length // 2
    freq = np.where(mode <= half, mode, mode - half)
    angle = 2.0 * math.pi / length * (grid * freq % length)
    scaling = np.where((mode == 0) | (mode == half), math.sqrt(1.0 / length), math.sqrt(2.0 / length))
    return np.where(mode <= half, np.cos(angle), np.sin(angle)) * scaling


def make_tables(D, G, XL, YL, Z):
    N, Y, KB, XP = D * XL, G * YL, Z // G, XL // G
    cz = cosine_table(Z)
    full = np.zeros((G, Z, G, G, KB))
    for g in range(G):
        for h in range(G):
            full[h, :, g, h, :] = cz[:, g * KB : (g + 1) * KB]
    full = full.reshape(G * Z, G * Z)
    mode = np.arange(Y)
    freq = np.where(mode <= Y // 2, mode, mode - Y // 2)
    eig_y = 2.0 * np.cos(2.0 * math.pi / Y * freq) - 2.0
    eig_z = 2.0 * np.cos(math.pi / Z * np.arange(Z)) - 2.0
    half_b = 1.0 - 0.5 * (eig_z[:, None] + eig_y[None, :])
    half_b[0, 0] = 2.0
    q = np.exp(-np.arccosh(half_b))
    factor = -q / (1.0 - q * q)
    q[0, 0] = 0.0
    factor[0, 0] = 0.0
    jump = q**XL
    wrap = 1.0 / (1.0 - q**N)
    ch = 2 * KB * Y // (128 * D)

    def tiles(table):
        blocks = []
        for g in range(G):
            rows = table[g * KB : (g + 1) * KB]
            part = [
                rows[k : k + ch, c : c + 128] for c in range(0, Y, 128) for k in range(0, KB, ch)
            ]
            blocks.append(np.stack(part + part))
        return np.stack(blocks).astype(np.float32)

    dist = np.arange(N)
    green = dist / 2.0 - dist * dist / (2.0 * N)
    green = green - green.mean()
    spot = (np.arange(N)[None, None, :] - XL * np.arange(D)[:, None, None] - np.arange(XL)[None, :, None]) % N
    z = np.arange(Z)
    band = np.zeros((Z, 3 * Z))
    for offset, c, d in zip(range(-3, 4), (-1, 9, -45, 0, 45, -9, 1), (1, -6, 15, -20, 15, -6, 1)):
        for k in range(Z):
            if 0 <= k + offset < Z:
                band[k + offset, k] = c
                band[k + offset, Z + k] = d
                if abs(offset) == 1:
                    band[k + offset, 2 * Z + k] = 1.0
    return (
        band.astype(ml_dtypes.bfloat16),
        *split_table(full),
        *split_table(fourier_table(Y)),
        q.reshape(G, KB, Y).astype(np.float32),
        factor.reshape(G, KB, Y).astype(np.float32),
        tiles(jump),
        tiles(wrap),
        green[spot].astype(np.float32),
    )


def two(value):
    high = value.astype(bf16)
    return high, (value - high.astype(f32)).astype(bf16)


def dot(a, b):
    return jnp.dot(a, b, preferred_element_type=f32)


def dot_nt(a, b):
    return lax.dot_general(a, b, (((1,), (1,)), ((), ())), preferred_element_type=f32)


def kernel(D, G, XL, YL, Z, *refs):
    (vx, vy, vz, temp, water, band, full_h, full_l, four_h, four_l, q_ref, fac_ref, jump, wrap, green,
     out_x, out_y, out_z, out_t, out_w, out_p,
     pad, zbuf, edge, ysend, xhalo, yhalo, corner, sx, sy, src,
     snd, got, spec, ends, ends_in, carry, carry_in, cplane, back, back_in,
     halo_send, halo_recv, gy_send, gy_recv, end_send, end_recv, car_send, car_recv, ret_send, ret_recv) = refs
    fields = (vx, vy, vz, temp, water)
    N, Y, KB, XP = D * XL, G * YL, Z // G, XL // G
    ch = carry.shape[1]
    H = D // 2
    ix, iy = lax.axis_index("gx"), lax.axis_index("gy")
    right, left = lax.rem(ix + 1, D), lax.rem(ix + D - 1, D)
    above, below = lax.rem(iy + 1, G), lax.rem(iy + G - 1, G)
    gx_peers = [lax.rem(ix + step, D) for step in range(1, D)]
    gy_peers = [lax.rem(iy + step, G) for step in range(1, G)]

    barrier = pltpu.get_barrier_semaphore()
    known = [(peer, iy) for peer in gx_peers] + [(ix, peer) for peer in gy_peers]
    known += [(right, above), (right, below), (left, above), (left, below)]
    for device in known:
        pl.semaphore_signal(barrier, inc=1, device_id=device, device_id_type=MESH)

    for f in range(5):
        for x in range(XL):
            edge[0, f, 4 * x : 4 * x + 4, :] = fields[f][x, 0:16, :].astype(f32)[0:4]
            edge[1, f, 4 * x : 4 * x + 4, :] = fields[f][x, YL - 16 : YL, :].astype(f32)[12:16]
    ysend[...] = edge[...].astype(bf16)
    pl.semaphore_wait(barrier, len(known))

    def remote(src_ref, dst_ref, send, recv, device):
        copy = pltpu.make_async_remote_copy(
            src_ref=src_ref, dst_ref=dst_ref, send_sem=send, recv_sem=recv,
            device_id=device, device_id_type=MESH,
        )
        copy.start()
        return copy

    halos = []

    def halo(src_ref, dst_ref, device):
        slot = len(halos)
        halos.append(remote(src_ref, dst_ref, halo_send.at[slot], halo_recv.at[slot], device))

    lines = 4 * XL
    for f in range(5):
        halo(fields[f].at[XL - 4 : XL], xhalo.at[0, f], (right, iy))
        halo(fields[f].at[0:4], xhalo.at[1, f], (left, iy))
    halo(ysend.at[1], yhalo.at[0], (ix, above))
    halo(ysend.at[0], yhalo.at[1], (ix, below))
    halo(ysend.at[1, :, lines - 16 : lines], corner.at[0], (right, above))
    halo(ysend.at[0, :, lines - 16 : lines], corner.at[1], (right, below))
    halo(ysend.at[1, :, 0:16], corner.at[2], (left, above))
    halo(ysend.at[0, :, 0:16], corner.at[3], (left, below))

    for f in range(5):
        pad[f, :, 0:8, :] = jnp.zeros((XL + 8, 8, Z), f32)
        pad[f, :, YL + 8 : YL + 16, :] = jnp.zeros((XL + 8, 8, Z), f32)
        pad[f, 4 : XL + 4, 8 : YL + 8, :] = fields[f][...].astype(f32)
    for copy in halos:
        copy.wait()
    for f in range(5):
        pad[f, 0:4, 8 : YL + 8, :] = xhalo[0, f].astype(f32)
        pad[f, XL + 4 : XL + 8, 8 : YL + 8, :] = xhalo[1, f].astype(f32)
        for side, row in ((0, 4), (1, YL + 8)):
            strip = yhalo[side, f].astype(f32)
            for x in range(XL):
                pad[f, 4 + x, row : row + 4, :] = strip[4 * x : 4 * x + 4]
            for far, start in ((0, 0), (2, XL + 4)):
                strip_c = corner[far + side, f].astype(f32)
                for x in range(4):
                    pad[f, start + x, row : row + 4, :] = strip_c[4 * x : 4 * x + 4]

    group = (XL + 8) // 4

    def along_z(f):
        def step(i, _):
            planes = pad[f, pl.ds(i * group, group)]
            rows = planes.reshape(group * (YL + 16), Z).astype(bf16)
            zbuf[pl.ds(i * group, group)] = dot(rows, band[...]).reshape(group, YL + 16, 3 * Z)
            return 0

        lax.fori_loop(0, 4, step, 0)

    def star(f, px, start, rows):
        low = 8 + start
        here = pl.ds(low, rows)
        centre = pad[f, px, here, :]
        sums = zbuf[px, here, 2 * Z : 3 * Z]
        speed = pad[2, px, here, :]
        total = speed * zbuf[px, here, 0:Z] - jnp.abs(speed) * zbuf[px, here, Z : 2 * Z]
        for axis in range(2):
            if axis == 0:
                get = lambda s: pad[f, px + s, here, :]
            else:
                get = lambda s: pad[f, px, pl.ds(low + s, rows), :]
            m1, p1, m2, p2, m3, p3 = get(-1), get(1), get(-2), get(2), get(-3), get(3)
            one = m1 + p1
            central = 45.0 * (p1 - m1) - 9.0 * (p2 - m2) + (p3 - m3)
            damped = 15.0 * one - 6.0 * (m2 + p2) + (m3 + p3) - 20.0 * centre
            speed = pad[axis, px, here, :]
            total = total + (speed * central - jnp.abs(speed) * damped)
            sums = sums + one
        result = centre + (time_step * diffusion) * (sums - 6.0 * centre) - (time_step / 60.0) * total
        if f == 2:
            result = result + time_step * pad[3, px, here, :]
        return result

    along_z(0)

    def step_x(x, _):
        for start in range(0, YL, 16):
            sx[x, start : start + 16, :] = star(0, x + 3, start, 16)
        return 0

    lax.fori_loop(0, XL + 2, step_x, 0)
    along_z(1)

    def step_y(x, _):
        for start in range(-1, YL - 16, 16):
            sy[x, start + 8 : start + 24, :] = star(1, x + 4, start, 16)
        sy[x, YL + 1 : YL + 9, :] = star(1, x + 4, YL - 7, 8)
        return 0

    lax.fori_loop(0, XL, step_y, 0)
    along_z(2)
    lane = lax.broadcasted_iota(jnp.int32, (16, Z), 1)

    def step_z(x, _):
        for start in range(0, YL, 16):
            here = pl.ds(start, 16)
            value = star(2, x + 4, start, 16)
            out_z[x, here, :] = value.astype(bf16)
            out_x[x, here, :] = sx[x + 1, here, :].astype(bf16)
            out_y[x, here, :] = sy[x, pl.ds(start + 8, 16), :].astype(bf16)
            up = jnp.where(lane < Z - 1, pltpu.roll(value, Z - 1, 1), 0.0)
            down = jnp.where(lane > 0, pltpu.roll(value, 1, 1), 0.0)
            grad = (sx[x + 2, here, :] - sx[x, here, :]) + (up - down)
            grad = grad + (sy[x, pl.ds(start + 9, 16), :] - sy[x, pl.ds(start + 7, 16), :])
            src[x, here, :] = grad * (0.5 / time_step)
        return 0

    lax.fori_loop(0, XL, step_z, 0)

    lhs = [two(src[h * XP : (h + 1) * XP].reshape(XP * YL, Z)) for h in range(G)]
    for g in range(G):
        cols = slice(g * Z, (g + 1) * Z)
        part = jnp.zeros((XP * YL, Z), f32)
        for h in range(G):
            rows = slice(h * Z, (h + 1) * Z)
            high, low = lhs[h]
            part = part + dot(high, full_h[rows, cols]) + dot(high, full_l[rows, cols]) + dot(low, full_h[rows, cols])
        snd[g] = part.reshape(XP, YL, Z)
    mine = pl.ds(pl.multiple_of(iy * YL, YL), YL)
    copies = [
        remote(snd.at[peer], got.at[:, mine, :], gy_send.at[n], gy_recv.at[n], (ix, peer))
        for n, peer in enumerate(gy_peers)
    ]
    got[:, mine, :] = snd[iy]

    for f, target in ((3, out_t), (4, out_w)):
        along_z(f)

        def step_s(x, _):
            for start in range(0, YL, 16):
                target[x, start : start + 16, :] = star(f, x + 4, start, 16).astype(bf16)
            return 0

        lax.fori_loop(0, XL, step_s, 0)
    for copy in copies:
        copy.wait()

    def fourier(i, _):
        high, low = two(got[i].T)
        spec[i] = dot(high, four_h[...]) + dot(high, four_l[...]) + dot(low, four_h[...])
        return 0

    lax.fori_loop(0, XP, fourier, 0)

    def line(x):
        h, i = x // XP, x % XP
        return i, slice(h * KB, (h + 1) * KB)

    q = q_ref[iy]
    end_a = spec[line(0)]
    for x in range(1, XL):
        end_a = spec[line(x)] + q * end_a
    end_b = spec[line(XL - 1)]
    for x in range(XL - 2, -1, -1):
        end_b = spec[line(x)] + q * end_b
    share = jnp.zeros((1, N), f32)
    for x in range(XL):
        i, rows = line(x)
        share = share + spec[i, rows.start : rows.start + 1, 0:1] * green[ix, x : x + 1, :]
    row8 = lax.broadcasted_iota(jnp.int32, (8, 128), 0)
    extra = jnp.zeros((8, 128), f32)
    for r in range(N // 128):
        extra = extra + jnp.where(row8 == r, share[:, r * 128 : (r + 1) * 128], 0.0)
    blocks = [(c, k) for c in range(0, Y, 128) for k in range(0, KB, ch)]
    for n, (c, k) in enumerate(blocks):
        ends[n, 0:ch, :] = end_a[k : k + ch, c : c + 128]
        ends[H + n, 0:ch, :] = end_b[k : k + ch, c : c + 128]
    for n in range(D):
        if ch < 8:
            ends[n, ch:8, :] = jnp.zeros((8 - ch, 128), f32)
        ends[n, 8:16, :] = extra

    def slot_of(device, worker):
        return device + (worker // H) * (D - 1 - 2 * device)

    copies = []
    for n, peer in enumerate(gx_peers):
        copies.append(
            remote(ends.at[peer], ends_in.at[slot_of(ix, peer)], end_send.at[n], end_recv.at[n], (peer, iy))
        )
    ends_in[slot_of(ix, ix)] = ends[ix]
    for copy in copies:
        copy.wait()
    jump_t, wrap_t = jump[iy, ix], wrap[iy, ix]
    state = ends_in[0, 0:ch, :]
    whole = ends_in[0, 8:16, :]
    for s in range(1, D):
        state = ends_in[s, 0:ch, :] + jump_t * state
        whole = whole + ends_in[s, 8:16, :]
    state = state * wrap_t
    for s in range(D):
        carry[s] = state
        if s < D - 1:
            state = ends_in[s, 0:ch, :] + jump_t * state
    copies = []
    for n, peer in enumerate(gx_peers):
        copies.append(
            remote(carry.at[slot_of(peer, ix)], carry_in.at[ix], car_send.at[n], car_recv.at[n], (peer, iy))
        )
    carry_in[ix] = carry[slot_of(ix, ix)]
    column = jnp.zeros((XL, 1), f32)
    for r in range(N // 128):
        spot = lax.broadcasted_iota(jnp.int32, (XL, 128), 1) + r * 128
        want = lax.broadcasted_iota(jnp.int32, (XL, 128), 0) + ix * XL
        column = column + jnp.sum(jnp.where(spot == want, whole[r : r + 1, :], 0.0), axis=1, keepdims=True)
    first = (lax.broadcasted_iota(jnp.int32, (XL, 128), 1) + iy) == 0
    column = jnp.where(first, column, 0.0)
    for copy in copies:
        copy.wait()
    for n, (c, k) in enumerate(blocks):
        cplane[0, k : k + ch, c : c + 128] = carry_in[n]
        cplane[1, k : k + ch, c : c + 128] = carry_in[H + n]
    factor = fac_ref[iy]
    state = cplane[0]
    for x in range(XL):
        i, rows = line(x)
        state = spec[i, rows, :] + q * state
        snd_i = pl.ds(0, KB)
        back[x, snd_i, :] = state
    state = cplane[1]
    for x in range(XL - 1, -1, -1):
        i, rows = line(x)
        value = spec[i, rows, :]
        ahead = q * state
        state = value + ahead
        spec[i, rows, :] = factor * (back[x, 0:KB, :] + ahead)
        spec[i, rows.start : rows.start + 1, 0:128] += column[x : x + 1, :]

    slabs = got

    def unfourier(i, _):
        high, low = two(spec[i])
        slabs[i] = dot_nt(four_h[...], high) + dot_nt(four_h[...], low) + dot_nt(four_l[...], high)
        return 0

    lax.fori_loop(0, XP, unfourier, 0)
    copies = []
    for n, peer in enumerate(gy_peers):
        part = pl.ds(pl.multiple_of(peer * YL, YL), YL)
        copies.append(
            remote(slabs.at[:, part, :], back_in.at[iy], ret_send.at[n], ret_recv.at[n], (ix, peer))
        )
    back_in[iy] = slabs[:, mine, :]
    for copy in copies:
        copy.wait()
    rhs = [two(back_in[g].reshape(XP * YL, Z)) for g in range(G)]
    for h in range(G):
        rows = slice(h * Z, (h + 1) * Z)
        part = jnp.zeros((XP * YL, Z), f32)
        for g in range(G):
            cols = slice(g * Z, (g + 1) * Z)
            high, low = rhs[g]
            part = part + dot_nt(high, full_h[rows, cols]) + dot_nt(high, full_l[rows, cols]) + dot_nt(low, full_h[rows, cols])
        out_p[h * XP : (h + 1) * XP] = part.reshape(XP, YL, Z)


def body(D, G, velocity_x, velocity_y, velocity_z, potential_temp, total_water):
    XL, YL, Z = velocity_x.shape
    Y, KB, XP = G * YL, Z // G, XL // G
    ch = 2 * KB * Y // (128 * D)
    tables = [jnp.asarray(t) for t in make_tables(D, G, XL, YL, Z)]
    dma = pltpu.SemaphoreType.DMA
    V = pltpu.VMEM
    scratch = [
        V((5, XL + 8, YL + 16, Z), f32),
        V((XL + 8, YL + 16, 3 * Z), f32),
        V((2, 5, 4 * XL, Z), f32),
        V((2, 5, 4 * XL, Z), bf16),
        V((2, 5, 4, YL, Z), bf16),
        V((2, 5, 4 * XL, Z), bf16),
        V((4, 5, 16, Z), bf16),
        V((XL + 2, YL, Z), f32),
        V((XL, YL + 16, Z), f32),
        V((XL, YL, Z), f32),
        V((G, XP, YL, Z), f32),
        V((XP, Y, Z), f32),
        V((XP, Z, Y), f32),
        V((D, 16, 128), f32),
        V((D, 16, 128), f32),
        V((D, ch, 128), f32),
        V((D, ch, 128), f32),
        V((2, KB, Y), f32),
        V((XL, KB, Y), f32),
        V((G, XP, YL, Z), f32),
        dma((16,)), dma((16,)),
        dma((G,)), dma((G,)),
        dma((D,)), dma((D,)),
        dma((D,)), dma((D,)),
        dma((G,)), dma((G,)),
    ]
    block = jax.ShapeDtypeStruct((XL, YL, Z), bf16)
    vmem = pl.BlockSpec(memory_space=pltpu.VMEM)
    return pl.pallas_call(
        functools.partial(kernel, D, G, XL, YL, Z),
        out_shape=(block,) * 5 + (jax.ShapeDtypeStruct((XL, YL, Z), f32),),
        in_specs=[vmem] * (5 + len(tables)),
        out_specs=(vmem,) * 6,
        scratch_shapes=scratch,
        compiler_params=pltpu.CompilerParams(
            collective_id=0, has_side_effects=True, vmem_limit_bytes=56 * 1024 * 1024
        ),
    )(velocity_x, velocity_y, velocity_z, potential_temp, total_water, *tables)


def solution(mesh):
    spec = P("gx", "gy", None)
    return jax.shard_map(
        functools.partial(body, mesh.shape["gx"], mesh.shape["gy"]),
        mesh=mesh,
        in_specs=(spec,) * 5,
        out_specs=(spec,) * 6,
        check_vma=False,
    )
```

```python
import functools
import math

import jax
import jax.numpy as jnp
import ml_dtypes
import numpy as np
from jax import lax
from jax.experimental import pallas as pl
from jax.experimental.pallas import tpu as pltpu
from jax.sharding import PartitionSpec as P

time_step = 0.25
diffusion = 0.1
f32 = jnp.float32
bf16 = jnp.bfloat16
MESH = pl.DeviceIdType.MESH


def split_table(table):
    high = table.astype(ml_dtypes.bfloat16)
    low = (table - high.astype(np.float64)).astype(ml_dtypes.bfloat16)
    return high, low


def cosine_table(length):
    grid = np.arange(length)[:, None]
    mode = np.arange(length)[None, :]
    scaling = np.where(mode == 0, math.sqrt(1.0 / length), math.sqrt(2.0 / length))
    return np.cos(math.pi / (2.0 * length) * (mode * (2 * grid + 1) % (4 * length))) * scaling


def fourier_table(length):
    grid = np.arange(length)[:, None]
    mode = np.arange(length)[None, :]
    half = length // 2
    freq = np.where(mode <= half, mode, mode - half)
    angle = 2.0 * math.pi / length * (grid * freq % length)
    scaling = np.where((mode == 0) | (mode == half), math.sqrt(1.0 / length), math.sqrt(2.0 / length))
    return np.where(mode <= half, np.cos(angle), np.sin(angle)) * scaling


def make_tables(D, G, XL, YL, Z):
    N, Y, KB, XP = D * XL, G * YL, Z // G, XL // G
    cz = cosine_table(Z)
    full = np.zeros((G, Z, G, G, KB))
    for g in range(G):
        for h in range(G):
            full[h, :, g, h, :] = cz[:, g * KB : (g + 1) * KB]
    full = full.reshape(G * Z, G * Z)
    mode = np.arange(Y)
    freq = np.where(mode <= Y // 2, mode, mode - Y // 2)
    eig_y = 2.0 * np.cos(2.0 * math.pi / Y * freq) - 2.0
    eig_z = 2.0 * np.cos(math.pi / Z * np.arange(Z)) - 2.0
    half_b = 1.0 - 0.5 * (eig_z[:, None] + eig_y[None, :])
    half_b[0, 0] = 2.0
    q = np.exp(-np.arccosh(half_b))
    factor = -q / (1.0 - q * q)
    q[0, 0] = 0.0
    factor[0, 0] = 0.0
    jump = q**XL
    wrap = 1.0 / (1.0 - q**N)
    ch = 2 * KB * Y // (128 * D)

    def tiles(table):
        blocks = []
        for g in range(G):
            rows = table[g * KB : (g + 1) * KB]
            part = [
                rows[k : k + ch, c : c + 128] for c in range(0, Y, 128) for k in range(0, KB, ch)
            ]
            blocks.append(np.stack(part + part))
        return np.stack(blocks).astype(np.float32)

    dist = np.arange(N)
    green = dist / 2.0 - dist * dist / (2.0 * N)
    green = green - green.mean()
    spot = (np.arange(N)[None, None, :] - XL * np.arange(D)[:, None, None] - np.arange(XL)[None, :, None]) % N
    z = np.arange(Z)
    band = np.zeros((Z, 3 * Z))
    for offset, c, d in zip(range(-3, 4), (-1, 9, -45, 0, 45, -9, 1), (1, -6, 15, -20, 15, -6, 1)):
        for k in range(Z):
            if 0 <= k + offset < Z:
                band[k + offset, k] = c
                band[k + offset, Z + k] = d
                if abs(offset) == 1:
                    band[k + offset, 2 * Z + k] = 1.0
    return (
        band.astype(ml_dtypes.bfloat16),
        *split_table(full),
        *split_table(fourier_table(Y)),
        q.reshape(G, KB, Y).astype(np.float32),
        factor.reshape(G, KB, Y).astype(np.float32),
        tiles(jump),
        tiles(wrap),
        green[spot].astype(np.float32),
    )


def two(value):
    high = value.astype(bf16)
    return high, (value - high.astype(f32)).astype(bf16)


def dot(a, b):
    return jnp.dot(a, b, preferred_element_type=f32)


def dot_nt(a, b):
    return lax.dot_general(a, b, (((1,), (1,)), ((), ())), preferred_element_type=f32)


def kernel(D, G, XL, YL, Z, *refs):
    (vx, vy, vz, temp, water, band, full_h, full_l, four_h, four_l, q_ref, fac_ref, jump, wrap, green,
     out_x, out_y, out_z, out_t, out_w, back_in,
     pad, zbuf, edge, ysend, xhalo, yhalo, corner, sx, sy, src,
     snd, got, spec, ends, ends_in, extra_out, extra_in, carry, carry_in, cplane, back,
     halo_send, halo_recv, gy_send, gy_recv, end_send, end_recv, ext_send, ext_recv, car_send, car_recv, ret_send, ret_recv) = refs
    fields = (vx, vy, vz, temp, water)
    N, Y, KB, XP = D * XL, G * YL, Z // G, XL // G
    ch = carry.shape[1]
    H = D // 2
    ix, iy = lax.axis_index("gx"), lax.axis_index("gy")
    right, left = lax.rem(ix + 1, D), lax.rem(ix + D - 1, D)
    above, below = lax.rem(iy + 1, G), lax.rem(iy + G - 1, G)
    gx_peers = [lax.rem(ix + step, D) for step in range(1, D)]
    gy_peers = [lax.rem(iy + step, G) for step in range(1, G)]

    barrier = pltpu.get_barrier_semaphore()
    known = [(peer, iy) for peer in gx_peers] + [(ix, peer) for peer in gy_peers]
    known += [(right, above), (right, below), (left, above), (left, below)]
    for device in known:
        pl.semaphore_signal(barrier, inc=1, device_id=device, device_id_type=MESH)

    for f in range(5):
        for x in range(XL):
            edge[0, f, 4 * x : 4 * x + 4, :] = fields[f][x, 0:16, :].astype(f32)[0:4]
            edge[1, f, 4 * x : 4 * x + 4, :] = fields[f][x, YL - 16 : YL, :].astype(f32)[12:16]
    ysend[...] = edge[...].astype(bf16)
    pl.semaphore_wait(barrier, len(known))

    def remote(src_ref, dst_ref, send, recv, device):
        copy = pltpu.make_async_remote_copy(
            src_ref=src_ref, dst_ref=dst_ref, send_sem=send, recv_sem=recv,
            device_id=device, device_id_type=MESH,
        )
        copy.start()
        return copy

    halos = []

    def halo(src_ref, dst_ref, device):
        slot = len(halos)
        halos.append(remote(src_ref, dst_ref, halo_send.at[slot], halo_recv.at[slot], device))

    lines = 4 * XL
    for f in range(5):
        halo(fields[f].at[XL - 4 : XL], xhalo.at[0, f], (right, iy))
        halo(fields[f].at[0:4], xhalo.at[1, f], (left, iy))
    halo(ysend.at[1], yhalo.at[0], (ix, above))
    halo(ysend.at[0], yhalo.at[1], (ix, below))
    halo(ysend.at[1, :, lines - 16 : lines], corner.at[0], (right, above))
    halo(ysend.at[0, :, lines - 16 : lines], corner.at[1], (right, below))
    halo(ysend.at[1, :, 0:16], corner.at[2], (left, above))
    halo(ysend.at[0, :, 0:16], corner.at[3], (left, below))

    for f in range(5):
        pad[f, :, 0:8, :] = jnp.zeros((XL + 8, 8, Z), f32)
        pad[f, :, YL + 8 : YL + 16, :] = jnp.zeros((XL + 8, 8, Z), f32)
        pad[f, 4 : XL + 4, 8 : YL + 8, :] = fields[f][...].astype(f32)

        def along_z(i, _):
            rows = fields[f][pl.ds(i * 4, 4)].reshape(4 * YL, Z)
            zbuf[f, pl.ds(4 + i * 4, 4), 8 : YL + 8, :] = dot(rows, band[...]).reshape(4, YL, 3 * Z)
            return 0

        lax.fori_loop(0, XL // 4, along_z, 0)
    for copy in halos:
        copy.wait()
    for f in range(5):
        pad[f, 0:4, 8 : YL + 8, :] = xhalo[0, f].astype(f32)
        pad[f, XL + 4 : XL + 8, 8 : YL + 8, :] = xhalo[1, f].astype(f32)
        for side, row in ((0, 4), (1, YL + 8)):
            strip = yhalo[side, f].astype(f32)
            for x in range(XL):
                pad[f, 4 + x, row : row + 4, :] = strip[4 * x : 4 * x + 4]
            for far, start in ((0, 0), (2, XL + 4)):
                strip_c = corner[far + side, f].astype(f32)
                for x in range(4):
                    pad[f, start + x, row : row + 4, :] = strip_c[4 * x : 4 * x + 4]

    outer = jnp.concatenate([pad[0, 3, 8 : YL + 8, :], pad[0, XL + 4, 8 : YL + 8, :]], axis=0)
    outer = dot(outer.astype(bf16), band[...])
    zbuf[0, 3, 8 : YL + 8, :] = outer[0:YL]
    zbuf[0, XL + 4, 8 : YL + 8, :] = outer[YL:]
    for row in (0, YL + 8):
        outer = pad[1, 4 : XL + 4, row : row + 8, :].reshape(XL * 8, Z)
        zbuf[1, 4 : XL + 4, row : row + 8, :] = dot(outer.astype(bf16), band[...]).reshape(XL, 8, 3 * Z)

    def star(f, px, start, rows):
        low = 8 + start
        here = pl.ds(low, rows)
        centre = pad[f, px, here, :]
        sums = zbuf[f, px, here, 2 * Z : 3 * Z]
        speed = pad[2, px, here, :]
        total = speed * zbuf[f, px, here, 0:Z] - jnp.abs(speed) * zbuf[f, px, here, Z : 2 * Z]
        for axis in range(2):
            if axis == 0:
                get = lambda s: pad[f, px + s, here, :]
            else:
                get = lambda s: pad[f, px, pl.ds(low + s, rows), :]
            m1, p1, m2, p2, m3, p3 = get(-1), get(1), get(-2), get(2), get(-3), get(3)
            one = m1 + p1
            central = 45.0 * (p1 - m1) - 9.0 * (p2 - m2) + (p3 - m3)
            damped = 15.0 * one - 6.0 * (m2 + p2) + (m3 + p3) - 20.0 * centre
            speed = pad[axis, px, here, :]
            total = total + (speed * central - jnp.abs(speed) * damped)
            sums = sums + one
        result = centre + (time_step * diffusion) * (sums - 6.0 * centre) - (time_step / 60.0) * total
        if f == 2:
            result = result + time_step * pad[3, px, here, :]
        return result

    def step_x(x, _):
        for start in range(0, YL, 16):
            sx[x, start : start + 16, :] = star(0, x + 3, start, 16)
        return 0

    lax.fori_loop(0, XL + 2, step_x, 0)

    def step_y(x, _):
        for start in range(-1, YL - 16, 16):
            sy[x, start + 8 : start + 24, :] = star(1, x + 4, start, 16)
        sy[x, YL + 1 : YL + 9, :] = star(1, x + 4, YL - 7, 8)
        return 0

    lax.fori_loop(0, XL, step_y, 0)
    lane = lax.broadcasted_iota(jnp.int32, (16, Z), 1)

    def step_z(x, _):
        for start in range(0, YL, 16):
            here = pl.ds(start, 16)
            value = star(2, x + 4, start, 16)
            out_z[x, here, :] = value.astype(bf16)
            out_x[x, here, :] = sx[x + 1, here, :].astype(bf16)
            out_y[x, here, :] = sy[x, pl.ds(start + 8, 16), :].astype(bf16)
            up = jnp.where(lane < Z - 1, pltpu.roll(value, Z - 1, 1), 0.0)
            down = jnp.where(lane > 0, pltpu.roll(value, 1, 1), 0.0)
            grad = (sx[x + 2, here, :] - sx[x, here, :]) + (up - down)
            grad = grad + (sy[x, pl.ds(start + 9, 16), :] - sy[x, pl.ds(start + 7, 16), :])
            src[x, here, :] = grad * (0.5 / time_step)
        return 0

    lax.fori_loop(0, XL, step_z, 0)

    mine = pl.ds(pl.multiple_of(iy * YL, YL), YL)
    half = XP // 2
    copies = []
    for c in range(2):
        planes = slice(c * half, (c + 1) * half)
        lhs = [two(src[h * XP + c * half : h * XP + (c + 1) * half].reshape(half * YL, Z)) for h in range(G)]
        for g in range(G):
            cols = slice(g * Z, (g + 1) * Z)
            part = jnp.zeros((half * YL, Z), f32)
            for h in range(G):
                rows = slice(h * Z, (h + 1) * Z)
                high, low = lhs[h]
                part = part + dot(high, full_h[rows, cols]) + dot(high, full_l[rows, cols]) + dot(low, full_h[rows, cols])
            snd[g, planes] = part.reshape(half, YL, Z)
        copies.append([
            remote(snd.at[peer, planes], got.at[planes, mine, :], gy_send.at[c * G + n], gy_recv.at[c * G + n], (ix, peer))
            for n, peer in enumerate(gy_peers)
        ])
        got[planes, mine, :] = snd[iy, planes]

    def scalar(f, target, first, last):
        def step_s(x, _):
            for start in range(0, YL, 16):
                target[x, start : start + 16, :] = star(f, x + 4, start, 16).astype(bf16)
            return 0

        lax.fori_loop(first, last, step_s, 0)

    scalar(3, out_t, 0, XL)

    def fourier(i, _):
        high, low = two(got[i].T)
        spec[i] = dot(high, four_h[...]) + dot(high, four_l[...]) + dot(low, four_h[...])
        return 0

    for c in range(2):
        for copy in copies[c]:
            copy.wait()
        lax.fori_loop(c * half, (c + 1) * half, fourier, 0)

    def line(x):
        h, i = x // XP, x % XP
        return i, slice(h * KB, (h + 1) * KB)

    q = q_ref[iy]
    end_a = spec[line(0)]
    for x in range(1, XL):
        end_a = spec[line(x)] + q * end_a
    end_b = spec[line(XL - 1)]
    for x in range(XL - 2, -1, -1):
        end_b = spec[line(x)] + q * end_b
    share = jnp.zeros((1, N), f32)
    for x in range(XL):
        i, rows = line(x)
        share = share + spec[i, rows.start : rows.start + 1, 0:1] * green[ix, x : x + 1, :]
    row8 = lax.broadcasted_iota(jnp.int32, (8, 128), 0)
    extra = jnp.zeros((8, 128), f32)
    for r in range(N // 128):
        extra = extra + jnp.where(row8 == r, share[:, r * 128 : (r + 1) * 128], 0.0)
    blocks = [(c, k) for c in range(0, Y, 128) for k in range(0, KB, ch)]
    for n, (c, k) in enumerate(blocks):
        ends[n] = end_a[k : k + ch, c : c + 128]
        ends[H + n] = end_b[k : k + ch, c : c + 128]
    extra_out[...] = extra

    def slot_of(device, worker):
        return device + (worker // H) * (D - 1 - 2 * device)

    copies = []
    for n, peer in enumerate(gx_peers):
        copies.append(
            remote(ends.at[peer], ends_in.at[slot_of(ix, peer)], end_send.at[n], end_recv.at[n], (peer, iy))
        )
    extras = []
    for n, peer in enumerate(gx_peers):
        extras.append(remote(extra_out, extra_in.at[ix], ext_send.at[n], ext_recv.at[n], (peer, iy)))
    extra_in[ix] = extra
    ends_in[slot_of(ix, ix)] = ends[ix]
    scalar(4, out_w, 0, XL // 2)
    for copy in copies:
        copy.wait()
    jump_t, wrap_t = jump[iy, ix], wrap[iy, ix]
    state = ends_in[0]
    for s in range(1, D):
        state = ends_in[s] + jump_t * state
    state = state * wrap_t
    for s in range(D):
        carry[s] = state
        if s < D - 1:
            state = ends_in[s] + jump_t * state
    copies = []
    for n, peer in enumerate(gx_peers):
        copies.append(
            remote(carry.at[slot_of(peer, ix)], carry_in.at[ix], car_send.at[n], car_recv.at[n], (peer, iy))
        )
    carry_in[ix] = carry[slot_of(ix, ix)]
    scalar(4, out_w, XL // 2, XL)
    for copy in extras:
        copy.wait()
    whole = extra_in[0]
    for s in range(1, D):
        whole = whole + extra_in[s]
    column = jnp.zeros((XL, 1), f32)
    for r in range(N // 128):
        spot = lax.broadcasted_iota(jnp.int32, (XL, 128), 1) + r * 128
        want = lax.broadcasted_iota(jnp.int32, (XL, 128), 0) + ix * XL
        column = column + jnp.sum(jnp.where(spot == want, whole[r : r + 1, :], 0.0), axis=1, keepdims=True)
    first = (lax.broadcasted_iota(jnp.int32, (XL, 128), 1) + iy) == 0
    column = jnp.where(first, column, 0.0)
    for copy in copies:
        copy.wait()
    for n, (c, k) in enumerate(blocks):
        cplane[0, k : k + ch, c : c + 128] = carry_in[n]
        cplane[1, k : k + ch, c : c + 128] = carry_in[H + n]
    factor = fac_ref[iy]
    state = cplane[0]
    for x in range(XL):
        i, rows = line(x)
        state = spec[i, rows, :] + q * state
        back[x] = state
    state = cplane[1]
    for x in range(XL - 1, -1, -1):
        i, rows = line(x)
        value = spec[i, rows, :]
        ahead = q * state
        state = value + ahead
        spec[i, rows, :] = factor * (back[x] + ahead)
        spec[i, rows.start : rows.start + 1, 0:128] += column[x : x + 1, :]

    slabs = got

    copies = []
    for i in range(XP):
        high, low = two(spec[i])
        slabs[i] = dot_nt(four_h[...], high) + dot_nt(four_h[...], low) + dot_nt(four_l[...], high)
        for n, peer in enumerate(gy_peers):
            part = pl.ds(pl.multiple_of(peer * YL, YL), YL)
            slot = i * G + n
            copies.append(
                remote(slabs.at[i, part, :], back_in.at[iy, i], ret_send.at[slot], ret_recv.at[slot], (ix, peer))
            )
        back_in[iy, i] = slabs[i, mine, :]
    for copy in copies:
        copy.wait()


def finish(G, back_in, full_h, full_l, *refs):
    sources, (out_p, *targets), sems = refs[:5], refs[5:11], refs[11]
    copies = [pltpu.make_async_copy(a, b, sems.at[n]) for n, (a, b) in enumerate(zip(sources, targets))]
    for copy in copies:
        copy.start()
    _, XP, YL, Z = back_in.shape
    rhs = [two(back_in[g].reshape(XP * YL, Z)) for g in range(G)]
    for h in range(G):
        rows = slice(h * Z, (h + 1) * Z)
        part = jnp.zeros((XP * YL, Z), f32)
        for g in range(G):
            cols = slice(g * Z, (g + 1) * Z)
            high, low = rhs[g]
            part = part + dot_nt(high, full_h[rows, cols]) + dot_nt(high, full_l[rows, cols]) + dot_nt(low, full_h[rows, cols])
        out_p[h * XP : (h + 1) * XP] = part.reshape(XP, YL, Z)
    for copy in copies:
        copy.wait()


def body(D, G, velocity_x, velocity_y, velocity_z, potential_temp, total_water):
    XL, YL, Z = velocity_x.shape
    Y, KB, XP = G * YL, Z // G, XL // G
    ch = 2 * KB * Y // (128 * D)
    tables = [jnp.asarray(t) for t in make_tables(D, G, XL, YL, Z)]
    dma = pltpu.SemaphoreType.DMA
    V = pltpu.VMEM
    scratch = [
        V((5, XL + 8, YL + 16, Z), f32),
        V((5, XL + 8, YL + 16, 3 * Z), f32),
        V((2, 5, 4 * XL, Z), f32),
        V((2, 5, 4 * XL, Z), bf16),
        V((2, 5, 4, YL, Z), bf16),
        V((2, 5, 4 * XL, Z), bf16),
        V((4, 5, 16, Z), bf16),
        V((XL + 2, YL, Z), f32),
        V((XL, YL + 16, Z), f32),
        V((XL, YL, Z), f32),
        V((G, XP, YL, Z), f32),
        V((XP, Y, Z), f32),
        V((XP, Z, Y), f32),
        V((D, ch, 128), f32),
        V((D, ch, 128), f32),
        V((8, 128), f32),
        V((D, 8, 128), f32),
        V((D, ch, 128), f32),
        V((D, ch, 128), f32),
        V((2, KB, Y), f32),
        V((XL, KB, Y), f32),
        dma((16,)), dma((16,)),
        dma((2 * G,)), dma((2 * G,)),
        dma((D,)), dma((D,)),
        dma((D,)), dma((D,)),
        dma((D,)), dma((D,)),
        dma((XP * G,)), dma((XP * G,)),
    ]
    block = jax.ShapeDtypeStruct((XL, YL, Z), bf16)
    vmem = pl.BlockSpec(memory_space=pltpu.VMEM)
    where = pl.BlockSpec(memory_space=pl.ANY)
    *stars, modes = pl.pallas_call(
        functools.partial(kernel, D, G, XL, YL, Z),
        out_shape=(block,) * 5 + (jax.ShapeDtypeStruct((G, XP, YL, Z), f32),),
        in_specs=[vmem] * (5 + len(tables)),
        out_specs=(vmem,) * 6,
        scratch_shapes=scratch,
        compiler_params=pltpu.CompilerParams(
            collective_id=0, has_side_effects=True, vmem_limit_bytes=56 * 1024 * 1024
        ),
    )(velocity_x, velocity_y, velocity_z, potential_temp, total_water, *tables)
    pressure, *stars = pl.pallas_call(
        functools.partial(finish, G),
        out_shape=(jax.ShapeDtypeStruct((XL, YL, Z), f32),) + (block,) * 5,
        in_specs=[vmem] * 3 + [where] * 5,
        out_specs=(vmem,) + (where,) * 5,
        scratch_shapes=[dma((5,))],
        compiler_params=pltpu.CompilerParams(vmem_limit_bytes=40 * 1024 * 1024),
    )(modes, tables[1], tables[2], *stars)
    return (*stars, pressure)


def solution(mesh):
    spec = P("gx", "gy", None)
    return jax.shard_map(
        functools.partial(body, mesh.shape["gx"], mesh.shape["gy"]),
        mesh=mesh,
        in_specs=(spec,) * 5,
        out_specs=(spec,) * 6,
        check_vma=False,
    )
```

```python
import functools
import math

import jax
import jax.numpy as jnp
import ml_dtypes
import numpy as np
from jax import lax
from jax.experimental import pallas as pl
from jax.experimental.pallas import tpu as pltpu
from jax.sharding import PartitionSpec as P

time_step = 0.25
diffusion = 0.1
f32 = jnp.float32
bf16 = jnp.bfloat16
MESH = pl.DeviceIdType.MESH


def split_table(table):
    high = table.astype(ml_dtypes.bfloat16)
    low = (table - high.astype(np.float64)).astype(ml_dtypes.bfloat16)
    return high, low


def cosine_table(length):
    grid = np.arange(length)[:, None]
    mode = np.arange(length)[None, :]
    scaling = np.where(mode == 0, math.sqrt(1.0 / length), math.sqrt(2.0 / length))
    return np.cos(math.pi / (2.0 * length) * (mode * (2 * grid + 1) % (4 * length))) * scaling


def fourier_table(length):
    grid = np.arange(length)[:, None]
    mode = np.arange(length)[None, :]
    half = length // 2
    freq = np.where(mode <= half, mode, mode - half)
    angle = 2.0 * math.pi / length * (grid * freq % length)
    scaling = np.where((mode == 0) | (mode == half), math.sqrt(1.0 / length), math.sqrt(2.0 / length))
    return np.where(mode <= half, np.cos(angle), np.sin(angle)) * scaling


def make_tables(D, G, XL, YL, Z):
    N, Y, KB, XP = D * XL, G * YL, Z // G, XL // G
    cz = cosine_table(Z)
    full = np.zeros((G, Z, G, G, KB))
    for g in range(G):
        for h in range(G):
            full[h, :, g, h, :] = cz[:, g * KB : (g + 1) * KB]
    full = full.reshape(G * Z, G * Z)
    mode = np.arange(Y)
    freq = np.where(mode <= Y // 2, mode, mode - Y // 2)
    eig_y = 2.0 * np.cos(2.0 * math.pi / Y * freq) - 2.0
    eig_z = 2.0 * np.cos(math.pi / Z * np.arange(Z)) - 2.0
    half_b = 1.0 - 0.5 * (eig_z[:, None] + eig_y[None, :])
    half_b[0, 0] = 2.0
    q = np.exp(-np.arccosh(half_b))
    factor = -q / (1.0 - q * q)
    q[0, 0] = 0.0
    factor[0, 0] = 0.0
    jump = q**XL
    wrap = 1.0 / (1.0 - q**N)
    ch = 2 * KB * Y // (128 * D)

    def tiles(table):
        blocks = []
        for g in range(G):
            rows = table[g * KB : (g + 1) * KB]
            part = [
                rows[k : k + ch, c : c + 128] for c in range(0, Y, 128) for k in range(0, KB, ch)
            ]
            blocks.append(np.stack(part + part))
        return np.stack(blocks).astype(np.float32)

    dist = np.arange(N)
    green = dist / 2.0 - dist * dist / (2.0 * N)
    green = green - green.mean()
    spot = (np.arange(N)[None, None, :] - XL * np.arange(D)[:, None, None] - np.arange(XL)[None, :, None]) % N
    z = np.arange(Z)
    band = np.zeros((Z, 3 * Z))
    for offset, c, d in zip(range(-3, 4), (-1, 9, -45, 0, 45, -9, 1), (1, -6, 15, -20, 15, -6, 1)):
        for k in range(Z):
            if 0 <= k + offset < Z:
                band[k + offset, k] = c
                band[k + offset, Z + k] = d
                if abs(offset) == 1:
                    band[k + offset, 2 * Z + k] = 1.0
    return (
        band.astype(ml_dtypes.bfloat16),
        *split_table(full),
        *split_table(fourier_table(Y)),
        q.reshape(G, KB, Y).astype(np.float32),
        factor.reshape(G, KB, Y).astype(np.float32),
        tiles(jump),
        tiles(wrap),
        green[spot].astype(np.float32),
    )


def two(value):
    high = value.astype(bf16)
    return high, (value - high.astype(f32)).astype(bf16)


def dot(a, b):
    return jnp.dot(a, b, preferred_element_type=f32)


def dot_nt(a, b):
    return lax.dot_general(a, b, (((1,), (1,)), ((), ())), preferred_element_type=f32)


def kernel(D, G, XL, YL, Z, *refs):
    (vx, vy, vz, temp, water, band, full_h, full_l, four_h, four_l, q_ref, fac_ref, jump, wrap, green,
     out_x, out_y, out_z, out_t, out_w, back_in,
     pad, zbuf, edge, ysend, xhalo, yhalo, corner, sx, sy, src,
     snd, got, spec, ends, ends_in, extra_out, extra_in, carry, carry_in, cplane, back,
     halo_send, halo_recv, gy_send, gy_recv, end_send, end_recv, ext_send, ext_recv, car_send, car_recv, ret_send, ret_recv) = refs
    fields = (vx, vy, vz, temp, water)
    N, Y, KB, XP = D * XL, G * YL, Z // G, XL // G
    ch = carry.shape[1]
    H = D // 2
    ix, iy = lax.axis_index("gx"), lax.axis_index("gy")
    right, left = lax.rem(ix + 1, D), lax.rem(ix + D - 1, D)
    above, below = lax.rem(iy + 1, G), lax.rem(iy + G - 1, G)
    gx_peers = [lax.rem(ix + step, D) for step in range(1, D)]
    gy_peers = [lax.rem(iy + step, G) for step in range(1, G)]

    barrier = pltpu.get_barrier_semaphore()
    known = [(peer, iy) for peer in gx_peers] + [(ix, peer) for peer in gy_peers]
    known += [(right, above), (right, below), (left, above), (left, below)]
    for device in known:
        pl.semaphore_signal(barrier, inc=1, device_id=device, device_id_type=MESH)

    for f in range(5):
        for x in range(XL):
            edge[0, f, 4 * x : 4 * x + 4, :] = fields[f][x, 0:16, :].astype(f32)[0:4]
            edge[1, f, 4 * x : 4 * x + 4, :] = fields[f][x, YL - 16 : YL, :].astype(f32)[12:16]
    ysend[...] = edge[...].astype(bf16)
    pl.semaphore_wait(barrier, len(known))

    def remote(src_ref, dst_ref, send, recv, device):
        copy = pltpu.make_async_remote_copy(
            src_ref=src_ref, dst_ref=dst_ref, send_sem=send, recv_sem=recv,
            device_id=device, device_id_type=MESH,
        )
        copy.start()
        return copy

    halos = []

    def halo(src_ref, dst_ref, device):
        slot = len(halos)
        halos.append(remote(src_ref, dst_ref, halo_send.at[slot], halo_recv.at[slot], device))

    lines = 4 * XL
    halo(ysend.at[1, 0:3], yhalo.at[0, 0:3], (ix, above))
    halo(ysend.at[0, 0:3], yhalo.at[1, 0:3], (ix, below))
    halo(ysend.at[1, 0:3, lines - 16 : lines], corner.at[0], (right, above))
    halo(ysend.at[0, 0:3, lines - 16 : lines], corner.at[1], (right, below))
    halo(ysend.at[1, 0:3, 0:16], corner.at[2], (left, above))
    halo(ysend.at[0, 0:3, 0:16], corner.at[3], (left, below))
    for f in range(3):
        halo(fields[f].at[XL - 4 : XL], xhalo.at[0, f], (right, iy))
        halo(fields[f].at[0:4], xhalo.at[1, f], (left, iy))
    wind_halos = len(halos)
    halo(ysend.at[1, 3:5], yhalo.at[0, 3:5], (ix, above))
    halo(ysend.at[0, 3:5], yhalo.at[1, 3:5], (ix, below))
    for f in range(3, 5):
        halo(fields[f].at[XL - 4 : XL], xhalo.at[0, f], (right, iy))
        halo(fields[f].at[0:4], xhalo.at[1, f], (left, iy))

    for f in range(5):
        pad[f, :, 0:8, :] = jnp.zeros((XL + 8, 8, Z), f32)
        pad[f, :, YL + 8 : YL + 16, :] = jnp.zeros((XL + 8, 8, Z), f32)
        pad[f, 4 : XL + 4, 8 : YL + 8, :] = fields[f][...].astype(f32)

        def along_z(i, _):
            rows = fields[f][pl.ds(i * 4, 4)].reshape(4 * YL, Z)
            zbuf[f, pl.ds(4 + i * 4, 4), 8 : YL + 8, :] = dot(rows, band[...]).reshape(4, YL, 3 * Z)
            return 0

        lax.fori_loop(0, XL // 4, along_z, 0)
    def unpack(f):
        pad[f, 0:4, 8 : YL + 8, :] = xhalo[0, f].astype(f32)
        pad[f, XL + 4 : XL + 8, 8 : YL + 8, :] = xhalo[1, f].astype(f32)
        for side, row in ((0, 4), (1, YL + 8)):
            strip = yhalo[side, f].astype(f32)
            for x in range(XL):
                pad[f, 4 + x, row : row + 4, :] = strip[4 * x : 4 * x + 4]
            if f < 3:
                for far, start in ((0, 0), (2, XL + 4)):
                    strip_c = corner[far + side, f].astype(f32)
                    for x in range(4):
                        pad[f, start + x, row : row + 4, :] = strip_c[4 * x : 4 * x + 4]

    for copy in halos[:wind_halos]:
        copy.wait()
    for f in range(3):
        unpack(f)
    outer = jnp.concatenate([pad[0, 3, 8 : YL + 8, :], pad[0, XL + 4, 8 : YL + 8, :]], axis=0)
    outer = dot(outer.astype(bf16), band[...])
    zbuf[0, 3, 8 : YL + 8, :] = outer[0:YL]
    zbuf[0, XL + 4, 8 : YL + 8, :] = outer[YL:]
    for row in (0, YL + 8):
        outer = pad[1, 4 : XL + 4, row : row + 8, :].reshape(XL * 8, Z)
        zbuf[1, 4 : XL + 4, row : row + 8, :] = dot(outer.astype(bf16), band[...]).reshape(XL, 8, 3 * Z)

    def star(f, px, start, rows):
        low = 8 + start
        here = pl.ds(low, rows)
        centre = pad[f, px, here, :]
        sums = zbuf[f, px, here, 2 * Z : 3 * Z]
        speed = pad[2, px, here, :]
        total = speed * zbuf[f, px, here, 0:Z] - jnp.abs(speed) * zbuf[f, px, here, Z : 2 * Z]
        for axis in range(2):
            if axis == 0:
                get = lambda s: pad[f, px + s, here, :]
            else:
                get = lambda s: pad[f, px, pl.ds(low + s, rows), :]
            m1, p1, m2, p2, m3, p3 = get(-1), get(1), get(-2), get(2), get(-3), get(3)
            one = m1 + p1
            central = 45.0 * (p1 - m1) - 9.0 * (p2 - m2) + (p3 - m3)
            damped = 15.0 * one - 6.0 * (m2 + p2) + (m3 + p3) - 20.0 * centre
            speed = pad[axis, px, here, :]
            total = total + (speed * central - jnp.abs(speed) * damped)
            sums = sums + one
        result = centre + (time_step * diffusion) * (sums - 6.0 * centre) - (time_step / 60.0) * total
        if f == 2:
            result = result + time_step * pad[3, px, here, :]
        return result

    lane = lax.broadcasted_iota(jnp.int32, (16, Z), 1)
    parts = min(4, XP)
    half = XP // parts
    mine = pl.ds(pl.multiple_of(iy * YL, YL), YL)

    def winds(c):
        wide = half + 2 if c == 0 else half
        offset = 0 if c == 0 else c * half + 2

        def step_x(j, _):
            x = (j // wide) * XP + offset + j % wide
            for start in range(0, YL, 16):
                sx[x, start : start + 16, :] = star(0, x + 3, start, 16)
            return 0

        def step_y(j, _):
            x = (j // half) * XP + c * half + j % half
            for start in range(-1, YL - 16, 16):
                sy[x, start + 8 : start + 24, :] = star(1, x + 4, start, 16)
            sy[x, YL + 1 : YL + 9, :] = star(1, x + 4, YL - 7, 8)
            return 0

        def step_z(j, _):
            x = (j // half) * XP + c * half + j % half
            for start in range(0, YL, 16):
                here = pl.ds(start, 16)
                value = star(2, x + 4, start, 16)
                out_z[x, here, :] = value.astype(bf16)
                out_x[x, here, :] = sx[x + 1, here, :].astype(bf16)
                out_y[x, here, :] = sy[x, pl.ds(start + 8, 16), :].astype(bf16)
                up = jnp.where(lane < Z - 1, pltpu.roll(value, Z - 1, 1), 0.0)
                down = jnp.where(lane > 0, pltpu.roll(value, 1, 1), 0.0)
                grad = (sx[x + 2, here, :] - sx[x, here, :]) + (up - down)
                grad = grad + (sy[x, pl.ds(start + 9, 16), :] - sy[x, pl.ds(start + 7, 16), :])
                src[x, here, :] = grad * (0.5 / time_step)
            return 0

        lax.fori_loop(0, G * wide, step_x, 0)
        lax.fori_loop(0, G * half, step_y, 0)
        lax.fori_loop(0, G * half, step_z, 0)

    copies = []
    for c in range(parts):
        winds(c)
        planes = slice(c * half, (c + 1) * half)
        lhs = [two(src[h * XP + c * half : h * XP + (c + 1) * half].reshape(half * YL, Z)) for h in range(G)]
        for g in range(G):
            cols = slice(g * Z, (g + 1) * Z)
            part = jnp.zeros((half * YL, Z), f32)
            for h in range(G):
                rows = slice(h * Z, (h + 1) * Z)
                high, low = lhs[h]
                part = part + dot(high, full_h[rows, cols]) + dot(high, full_l[rows, cols]) + dot(low, full_h[rows, cols])
            snd[g, planes] = part.reshape(half, YL, Z)
        copies.append([
            remote(snd.at[peer, planes], got.at[planes, mine, :], gy_send.at[c * G + n], gy_recv.at[c * G + n], (ix, peer))
            for n, peer in enumerate(gy_peers)
        ])
        got[planes, mine, :] = snd[iy, planes]

    for copy in halos[wind_halos:]:
        copy.wait()
    for f in range(3, 5):
        unpack(f)

    def scalar(f, target, first, last):
        def step_s(x, _):
            for start in range(0, YL, 16):
                target[x, start : start + 16, :] = star(f, x + 4, start, 16).astype(bf16)
            return 0

        lax.fori_loop(first, last, step_s, 0)

    scalar(3, out_t, 0, XL // 2)

    def fourier(i, _):
        high, low = two(got[i].T)
        spec[i] = dot(high, four_h[...]) + dot(high, four_l[...]) + dot(low, four_h[...])
        return 0

    for c in range(parts):
        for copy in copies[c]:
            copy.wait()
        lax.fori_loop(c * half, (c + 1) * half, fourier, 0)

    def line(x):
        h, i = x // XP, x % XP
        return i, slice(h * KB, (h + 1) * KB)

    q = q_ref[iy]
    end_a = spec[line(0)]
    for x in range(1, XL):
        end_a = spec[line(x)] + q * end_a
    end_b = spec[line(XL - 1)]
    for x in range(XL - 2, -1, -1):
        end_b = spec[line(x)] + q * end_b
    share = jnp.zeros((1, N), f32)
    for x in range(XL):
        i, rows = line(x)
        share = share + spec[i, rows.start : rows.start + 1, 0:1] * green[ix, x : x + 1, :]
    row8 = lax.broadcasted_iota(jnp.int32, (8, 128), 0)
    extra = jnp.zeros((8, 128), f32)
    for r in range(N // 128):
        extra = extra + jnp.where(row8 == r, share[:, r * 128 : (r + 1) * 128], 0.0)
    blocks = [(c, k) for c in range(0, Y, 128) for k in range(0, KB, ch)]
    for n, (c, k) in enumerate(blocks):
        ends[n] = end_a[k : k + ch, c : c + 128]
        ends[H + n] = end_b[k : k + ch, c : c + 128]
    extra_out[...] = extra

    def slot_of(device, worker):
        return device + (worker // H) * (D - 1 - 2 * device)

    copies = []
    for n, peer in enumerate(gx_peers):
        copies.append(
            remote(ends.at[peer], ends_in.at[slot_of(ix, peer)], end_send.at[n], end_recv.at[n], (peer, iy))
        )
    extras = []
    for n, peer in enumerate(gx_peers):
        extras.append(remote(extra_out, extra_in.at[ix], ext_send.at[n], ext_recv.at[n], (peer, iy)))
    extra_in[ix] = extra
    ends_in[slot_of(ix, ix)] = ends[ix]
    scalar(3, out_t, XL // 2, XL)
    scalar(4, out_w, 0, XL // 4)
    for copy in copies:
        copy.wait()
    jump_t, wrap_t = jump[iy, ix], wrap[iy, ix]
    state = ends_in[0]
    for s in range(1, D):
        state = ends_in[s] + jump_t * state
    state = state * wrap_t
    for s in range(D):
        carry[s] = state
        if s < D - 1:
            state = ends_in[s] + jump_t * state
    copies = []
    for n, peer in enumerate(gx_peers):
        copies.append(
            remote(carry.at[slot_of(peer, ix)], carry_in.at[ix], car_send.at[n], car_recv.at[n], (peer, iy))
        )
    carry_in[ix] = carry[slot_of(ix, ix)]
    scalar(4, out_w, XL // 4, XL)
    for copy in extras:
        copy.wait()
    whole = extra_in[0]
    for s in range(1, D):
        whole = whole + extra_in[s]
    column = jnp.zeros((XL, 1), f32)
    for r in range(N // 128):
        spot = lax.broadcasted_iota(jnp.int32, (XL, 128), 1) + r * 128
        want = lax.broadcasted_iota(jnp.int32, (XL, 128), 0) + ix * XL
        column = column + jnp.sum(jnp.where(spot == want, whole[r : r + 1, :], 0.0), axis=1, keepdims=True)
    first = (lax.broadcasted_iota(jnp.int32, (XL, 128), 1) + iy) == 0
    column = jnp.where(first, column, 0.0)
    for copy in copies:
        copy.wait()
    for n, (c, k) in enumerate(blocks):
        cplane[0, k : k + ch, c : c + 128] = carry_in[n]
        cplane[1, k : k + ch, c : c + 128] = carry_in[H + n]
    factor = fac_ref[iy]
    state = cplane[0]
    for x in range(XL):
        i, rows = line(x)
        state = spec[i, rows, :] + q * state
        back[x] = state
    state = cplane[1]
    for x in range(XL - 1, -1, -1):
        i, rows = line(x)
        value = spec[i, rows, :]
        ahead = q * state
        state = value + ahead
        spec[i, rows, :] = factor * (back[x] + ahead)
        spec[i, rows.start : rows.start + 1, 0:128] += column[x : x + 1, :]

    slabs = got

    copies = []
    for i in range(XP):
        high, low = two(spec[i])
        slabs[i] = dot_nt(four_h[...], high) + dot_nt(four_h[...], low) + dot_nt(four_l[...], high)
        for n, peer in enumerate(gy_peers):
            part = pl.ds(pl.multiple_of(peer * YL, YL), YL)
            slot = i * G + n
            copies.append(
                remote(slabs.at[i, part, :], back_in.at[iy, i], ret_send.at[slot], ret_recv.at[slot], (ix, peer))
            )
        back_in[iy, i] = slabs[i, mine, :]
    for copy in copies:
        copy.wait()


def finish(G, back_in, full_h, full_l, *refs):
    sources, (out_p, *targets), held, came, left = refs[:5], refs[5:11], refs[11], refs[12], refs[13]
    fetched = [pltpu.make_async_copy(a, held.at[n], came.at[n]) for n, a in enumerate(sources)]
    copies = [pltpu.make_async_copy(held.at[n], b, left.at[n]) for n, b in enumerate(targets)]
    for copy in fetched:
        copy.start()
    for first, second in zip(fetched, copies):
        first.wait()
        second.start()
    _, XP, YL, Z = back_in.shape
    rhs = [two(back_in[g].reshape(XP * YL, Z)) for g in range(G)]
    for h in range(G):
        rows = slice(h * Z, (h + 1) * Z)
        part = jnp.zeros((XP * YL, Z), f32)
        for g in range(G):
            cols = slice(g * Z, (g + 1) * Z)
            high, low = rhs[g]
            part = part + dot_nt(high, full_h[rows, cols]) + dot_nt(high, full_l[rows, cols]) + dot_nt(low, full_h[rows, cols])
        out_p[h * XP : (h + 1) * XP] = part.reshape(XP, YL, Z)
    for copy in copies:
        copy.wait()


def body(D, G, velocity_x, velocity_y, velocity_z, potential_temp, total_water):
    XL, YL, Z = velocity_x.shape
    Y, KB, XP = G * YL, Z // G, XL // G
    ch = 2 * KB * Y // (128 * D)
    tables = [jnp.asarray(t) for t in make_tables(D, G, XL, YL, Z)]
    dma = pltpu.SemaphoreType.DMA
    V = pltpu.VMEM
    scratch = [
        V((5, XL + 8, YL + 16, Z), f32),
        V((5, XL + 8, YL + 16, 3 * Z), f32),
        V((2, 5, 4 * XL, Z), f32),
        V((2, 5, 4 * XL, Z), bf16),
        V((2, 5, 4, YL, Z), bf16),
        V((2, 5, 4 * XL, Z), bf16),
        V((4, 3, 16, Z), bf16),
        V((XL + 2, YL, Z), f32),
        V((XL, YL + 16, Z), f32),
        V((XL, YL, Z), f32),
        V((G, XP, YL, Z), f32),
        V((XP, Y, Z), f32),
        V((XP, Z, Y), f32),
        V((D, ch, 128), f32),
        V((D, ch, 128), f32),
        V((8, 128), f32),
        V((D, 8, 128), f32),
        V((D, ch, 128), f32),
        V((D, ch, 128), f32),
        V((2, KB, Y), f32),
        V((XL, KB, Y), f32),
        dma((18,)), dma((18,)),
        dma((4 * G,)), dma((4 * G,)),
        dma((D,)), dma((D,)),
        dma((D,)), dma((D,)),
        dma((D,)), dma((D,)),
        dma((XP * G,)), dma((XP * G,)),
    ]
    block = jax.ShapeDtypeStruct((XL, YL, Z), bf16)
    vmem = pl.BlockSpec(memory_space=pltpu.VMEM)
    where = pl.BlockSpec(memory_space=pltpu.HBM)
    *stars, modes = pl.pallas_call(
        functools.partial(kernel, D, G, XL, YL, Z),
        out_shape=(block,) * 5 + (jax.ShapeDtypeStruct((G, XP, YL, Z), f32),),
        in_specs=[vmem] * (5 + len(tables)),
        out_specs=(vmem,) * 6,
        scratch_shapes=scratch,
        compiler_params=pltpu.CompilerParams(
            collective_id=0, has_side_effects=True, vmem_limit_bytes=56 * 1024 * 1024
        ),
    )(velocity_x, velocity_y, velocity_z, potential_temp, total_water, *tables)
    pressure, *stars = pl.pallas_call(
        functools.partial(finish, G),
        out_shape=(jax.ShapeDtypeStruct((XL, YL, Z), f32),) + (block,) * 5,
        in_specs=[vmem] * 3 + [where] * 5,
        out_specs=(vmem,) + (where,) * 5,
        scratch_shapes=[V((5, XL, YL, Z), bf16), dma((5,)), dma((5,))],
        compiler_params=pltpu.CompilerParams(vmem_limit_bytes=60 * 1024 * 1024),
    )(modes, tables[1], tables[2], *stars)
    return (*stars, pressure)


def solution(mesh):
    spec = P("gx", "gy", None)
    return jax.shard_map(
        functools.partial(body, mesh.shape["gx"], mesh.shape["gy"]),
        mesh=mesh,
        in_specs=(spec,) * 5,
        out_specs=(spec,) * 6,
        check_vma=False,
    )
```
